1024 devices in a mesh: side: 2 (over x_hi), grp: 32 (over z, core), shard: 16 (over x_lo, y).
Axes of the slice: x: 4 (x_hi: 2, x_lo: 2; x = x_hi * 2 + x_lo), y: 8, z: 16, core: 2. Of those that a mesh axis runs over, the one named last changes fastest.
Arguments:
- gradient: float32 [64, 256, 512], P(('side', 'grp'), 'shard'), may hold values from -160 to 160
- momentum: float32 [64, 256, 512], P(('side', 'grp'), 'shard'), may hold values from -6 to 6
- master: float32 [64, 256, 512], P(('side', 'grp'), 'shard'), may hold values from -6 to 6
- clip_count: int32 [64], P(('side', 'grp')), may hold values from 0 to 4
- logit_peak: float32 [64], P(('side', 'grp')), may hold values from 150 to 600
- server_map: int32 [64], replicated, may hold values from 0 to 63, each once
Outputs:
- new_master: float32 [64, 256, 512], P(('side', 'grp'), 'shard')
- new_momentum: float32 [64, 256, 512], P(('side', 'grp'), 'shard')
- serving: bfloat16 [64, 256, 512], P('shard')
The draws below stay inside these ranges and needn't reach their ends.
All inputs are finite; a program needn't handle non-finite values.
Results may differ from the reference program's by a relative error of at most 0.006.
Values may be sent and summed in bfloat16 or wider, within the bound.
No kernel may reach another device: no remote copies, remote signals or barrier semaphores. Data moves between devices by JAX's collectives and lax.ppermute only.
A program may use at most 32 MiB of HBM per device.

```python
import math
import jax
import jax.numpy as jnp
from jax import lax

HEADS = 64
KVR = 512
HOUT = 256
K_NOPE = 128
ITERS = 5


def draw_gradient(key, part):
    key = jax.random.fold_in(key, 11)
    key_values = jax.random.fold_in(key, 1)
    key_rows = jax.random.fold_in(key, 2)
    key_cols = jax.random.fold_in(key, 3)
    values = jnp.clip(jax.random.normal(key_values, (HEADS, HOUT, KVR), jnp.float32), -6.0, 6.0)
    spread = math.log(10.0)
    row_scale = jnp.exp(jax.random.uniform(key_rows, (HEADS, HOUT, 1), jnp.float32, 0.0, spread))
    col_scale = jnp.exp(jax.random.uniform(key_cols, (HEADS, 1, KVR), jnp.float32, 0.0, spread))
    return (0.2 * values * row_scale * col_scale).astype(jnp.float32)


def touch_ends(values, key, smallest, top_value):
    longest = values.shape.index(max(values.shape))
    spots = []
    for shift in (0, 1):
        where = [jax.random.randint(jax.random.fold_in(key, axis), (), 0, length) for axis, length in enumerate(values.shape)]
        where[longest] = (where[longest] + shift) % values.shape[longest]
        spots.append(tuple(where))
    return values.at[spots[0]].set(smallest).at[spots[1]].set(top_value)


def level_of(own_key, shape, cuts, least, high):
    def one(position, blocks):
        heights = jax.random.uniform(jax.random.fold_in(jax.random.fold_in(own_key, 6), position), (blocks,), jnp.float32, least / len(cuts), high / len(cuts))
        return jnp.repeat(jnp.exp(heights), shape[position] // blocks).reshape((-1,) + (1,) * (len(shape) - position - 1))

    gain = one(*cuts[0])
    for cut in cuts[1:]:
        gain = gain * one(*cut)
    return gain


def normal_values(own_key, extent, deviation, limit, shards=(), dtype=jnp.bfloat16):
    entries = deviation * jax.random.normal(own_key, extent, jnp.float32)
    if shards:
        entries = entries * level_of(own_key, extent, shards, -0.22, 0.18)
    return jnp.clip(entries, -limit, limit).astype(dtype)


def setup_inputs(seed: int = 0) -> dict:
    keys = jax.random.split(jax.random.key(seed), 7)
    return {
        "gradient": draw_gradient(jax.random.fold_in(keys[6], 71), 0),
        "momentum": normal_values(keys[1], (HEADS, HOUT, KVR), 1.0, 6.0, ((0, 64), (1, 16)), jnp.float32),
        "master": normal_values(keys[2], (HEADS, HOUT, KVR), 1.0, 6.0, ((0, 64), (1, 16)), jnp.float32),
        "clip_count": touch_ends(jax.random.randint(keys[3], (HEADS,), 0, 5), jax.random.fold_in(keys[3], 1), 0, 4).astype(jnp.int32),
        "logit_peak": jnp.clip(jnp.exp(math.log(600.0) - 1.3862944 * jax.random.uniform(keys[4], (HEADS,), jnp.float32) ** level_of(keys[4], (HEADS,), ((0, 64),), -0.2, 0.2)), 150.0, 600.0),
        "server_map": jax.random.permutation(keys[5], HEADS).astype(jnp.int32),
    }


newton_a = 3.4445
newton_b = -4.775
newton_c = 2.0315
momentum_mu = 0.95
learn_rate = 0.5
decay_rate = 0.1
clip_tau = 100.0
epsilon = 1e-07
highest = lax.Precision.HIGHEST

def orthogonal(matrix):
    norm_value = jnp.sqrt(jnp.sum(matrix * matrix)) + epsilon
    current = matrix / norm_value
    for iteration in range(ITERS):
        gram = jnp.dot(current, current.T, precision=highest)
        poly = newton_b * gram + newton_c * jnp.dot(gram, gram, precision=highest)
        current = newton_a * current + jnp.dot(poly, current, precision=highest)
    return current

def reference(gradient, momentum, master, clip_count, logit_peak, server_map):
    new_momentum = momentum_mu * momentum + gradient
    nesterov = gradient + momentum_mu * new_momentum
    ortho = lax.map(orthogonal, nesterov)
    gamma = jnp.where(clip_count > 0, clip_tau / logit_peak, jnp.ones_like(logit_peak))
    row_index = jnp.arange(HOUT)
    factor = jnp.where(row_index[None, :, None] < K_NOPE, jnp.sqrt(gamma)[:, None, None], jnp.ones_like(gamma)[:, None, None])
    updated = ((1.0 - learn_rate * decay_rate) * master - learn_rate * 0.2 * math.sqrt(KVR) * ortho) * factor
    serving = jnp.take(updated.astype(jnp.bfloat16), server_map.astype(jnp.int32), axis=0)
    return (updated, new_momentum, serving)
```

```python
import math

import jax
import jax.numpy as jnp
from jax import lax
from jax.sharding import Mesh
from jax.sharding import PartitionSpec as P

KVR = 512
K_NOPE = 128
ITERS = 5


newton_a = 3.4445
newton_b = -4.775
newton_c = 2.0315
momentum_mu = 0.95
learn_rate = 0.5
decay_rate = 0.1
clip_tau = 100.0
epsilon = 1e-07
highest = lax.Precision.HIGHEST

HEAD_AXES = ("xh", "z", "core")
SHARD_AXIS = "shard"
PARTS = 4


def orthogonal(matrix):
    norm_value = jnp.sqrt(jnp.sum(matrix * matrix)) + epsilon
    current = matrix / norm_value
    for iteration in range(ITERS):
        gram = jnp.dot(current, current.T, precision=highest)
        poly = newton_b * gram + newton_c * jnp.dot(gram, gram, precision=highest)
        current = newton_a * current + jnp.dot(poly, current, precision=highest)
    return current


def shards(gradient, momentum, master, clip_count, logit_peak, server_map):
    new_momentum = momentum_mu * momentum + gradient
    nesterov = gradient + momentum_mu * new_momentum
    _, row_count, columns = gradient.shape
    shard_count = lax.axis_size(SHARD_AXIS)
    z_count = lax.axis_size("z")
    shard_pos = lax.axis_index(SHARD_AXIS)

    own_rows = jnp.broadcast_to(nesterov.astype(jnp.bfloat16), (shard_count, row_count, columns))
    whole_head = lax.all_to_all(own_rows, SHARD_AXIS, 0, 0, tiled=True)
    whole_head = whole_head.reshape(shard_count * row_count, columns).astype(jnp.float32)
    ortho_whole = orthogonal(whole_head)
    ortho_rows = lax.dynamic_slice_in_dim(ortho_whole, shard_pos * row_count, row_count, 0)[None]

    gamma = jnp.where(clip_count > 0, clip_tau / logit_peak, jnp.ones_like(logit_peak))
    row_index = shard_pos * row_count + jnp.arange(row_count, dtype=jnp.int32)
    factor = jnp.where(
        row_index[None, :, None] < K_NOPE,
        jnp.sqrt(gamma)[:, None, None],
        jnp.ones_like(gamma)[:, None, None],
    )
    updated = (
        (1.0 - learn_rate * decay_rate) * master - learn_rate * 0.2 * math.sqrt(KVR) * ortho_rows
    ) * factor

    part_width = columns // PARTS
    parts = updated[0].astype(jnp.bfloat16).reshape(row_count, 2, 2, part_width)
    parts = parts.transpose(2, 1, 0, 3)[:, None]
    sent = jnp.broadcast_to(parts, (2, z_count, 2, row_count, part_width))
    sent = sent.reshape(4 * z_count, row_count, part_width)
    head_parts = lax.all_to_all(sent, HEAD_AXES, 0, 0, tiled=True)
    ordered = jnp.take(head_parts, server_map, axis=0, mode="clip")
    serving = lax.all_to_all(ordered, SHARD_AXIS, split_axis=0, concat_axis=1, tiled=True)
    serving = lax.all_gather(serving, "xh", axis=2, tiled=True)
    serving = lax.all_gather(serving, "core", axis=2, tiled=True)
    return (updated, new_momentum, serving)


def solution(mesh):
    side, grp, shard = (mesh.shape[name] for name in ("side", "grp", "shard"))
    fine = Mesh(
        mesh.devices.reshape(side, grp // 2, 2, shard), ("xh", "z", "core", "shard")
    )
    rows = P(HEAD_AXES, SHARD_AXIS, None)
    return jax.shard_map(
        shards,
        mesh=fine,
        in_specs=(rows, rows, rows, P(HEAD_AXES), P(HEAD_AXES), P()),
        out_specs=(rows, rows, P(SHARD_AXIS, None, None)),
        check_vma=False,
    )
```

```python
import math

import jax
import jax.numpy as jnp
from jax import lax
from jax.sharding import Mesh
from jax.sharding import PartitionSpec as P

KVR = 512
K_NOPE = 128
ITERS = 5


newton_a = 3.4445
newton_b = -4.775
newton_c = 2.0315
momentum_mu = 0.95
learn_rate = 0.5
decay_rate = 0.1
clip_tau = 100.0
epsilon = 1e-07
highest = lax.Precision.HIGHEST

HEAD_AXES = ("xh", "z", "core")
SHARD_AXIS = "shard"
PARTS = 4


def orthogonal(matrix):
    norm_value = jnp.sqrt(jnp.sum(matrix * matrix)) + epsilon
    current = matrix / norm_value
    for iteration in range(ITERS):
        gram = jnp.dot(current, current.T, precision=highest)
        poly = newton_b * gram + newton_c * jnp.dot(gram, gram, precision=highest)
        current = newton_a * current + jnp.dot(poly, current, precision=highest)
    return current


def swap_join(own, axis):
    other = lax.ppermute(own, axis, [(0, 1), (1, 0)])
    first = lax.axis_index(axis) == 0
    return jnp.concatenate([jnp.where(first, own, other), jnp.where(first, other, own)], axis=2)


def shards(gradient, momentum, master, clip_count, logit_peak, server_map):
    new_momentum = momentum_mu * momentum + gradient
    nesterov = gradient + momentum_mu * new_momentum
    _, row_count, columns = gradient.shape
    shard_count = lax.axis_size(SHARD_AXIS)
    z_count = lax.axis_size("z")
    shard_pos = lax.axis_index(SHARD_AXIS)

    own_rows = jnp.broadcast_to(nesterov.astype(jnp.bfloat16), (shard_count, row_count, columns))
    whole_head = lax.all_to_all(own_rows, SHARD_AXIS, 0, 0, tiled=True)
    whole_head = whole_head.reshape(shard_count * row_count, columns).astype(jnp.float32)
    ortho_whole = orthogonal(whole_head)
    ortho_rows = lax.dynamic_slice_in_dim(ortho_whole, shard_pos * row_count, row_count, 0)[None]

    gamma = jnp.where(clip_count > 0, clip_tau / logit_peak, jnp.ones_like(logit_peak))
    row_index = shard_pos * row_count + jnp.arange(row_count, dtype=jnp.int32)
    factor = jnp.where(
        row_index[None, :, None] < K_NOPE,
        jnp.sqrt(gamma)[:, None, None],
        jnp.ones_like(gamma)[:, None, None],
    )
    updated = (
        (1.0 - learn_rate * decay_rate) * master - learn_rate * 0.2 * math.sqrt(KVR) * ortho_rows
    ) * factor

    part_width = columns // PARTS
    parts = updated[0].astype(jnp.bfloat16).reshape(row_count, PARTS, part_width).transpose(1, 0, 2)
    chip_parts = lax.all_to_all(parts, ("core", "xh"), 0, 0, tiled=True)
    sent = jnp.broadcast_to(chip_parts, (z_count, PARTS, row_count, part_width))
    head_parts = lax.all_to_all(sent, "z", 0, 0, tiled=True)
    head_parts = head_parts.reshape(z_count * PARTS, row_count, part_width)
    half = z_count * 2
    xh_of, z_of, core_of = server_map // half, (server_map % half) // 2, server_map % 2
    ordered = jnp.take(head_parts, z_of * PARTS + core_of * 2 + xh_of, axis=0, mode="clip")
    own = lax.all_to_all(ordered, SHARD_AXIS, split_axis=0, concat_axis=1, tiled=True)
    serving = swap_join(swap_join(own, "xh"), "core")
    return (updated, new_momentum, serving)


def solution(mesh):
    side, grp, shard = (mesh.shape[name] for name in ("side", "grp", "shard"))
    fine = Mesh(
        mesh.devices.reshape(side, grp // 2, 2, shard), ("xh", "z", "core", "shard")
    )
    rows = P(HEAD_AXES, SHARD_AXIS, None)
    return jax.shard_map(
        shards,
        mesh=fine,
        in_specs=(rows, rows, rows, P(HEAD_AXES), P(HEAD_AXES), P()),
        out_specs=(rows, rows, P(SHARD_AXIS, None, None)),
        check_vma=False,
    )
```

```python
import math

import jax
import jax.numpy as jnp
from jax import lax
from jax.experimental import pallas as pl
from jax.experimental.pallas import tpu as pltpu
from jax.sharding import Mesh
from jax.sharding import PartitionSpec as P

KVR = 512
K_NOPE = 128
ITERS = 5


newton_a = 3.4445
newton_b = -4.775
newton_c = 2.0315
momentum_mu = 0.95
learn_rate = 0.5
decay_rate = 0.1
clip_tau = 100.0
epsilon = 1e-07

HEAD_AXES = ("xh", "z", "core")
SHARD_AXIS = "shard"
PARTS = 4

VMEM = pl.BlockSpec(memory_space=pltpu.VMEM)
SMEM = pl.BlockSpec(memory_space=pltpu.SMEM)


def dot(left, right):
    return jnp.dot(left, right, preferred_element_type=jnp.float32)


def dot_t(left, right):
    return lax.dot_general(
        left, right, (((1,), (1,)), ((), ())), preferred_element_type=jnp.float32
    )


def split(value):
    high = value.astype(jnp.bfloat16)
    return high, (value - high.astype(jnp.float32)).astype(jnp.bfloat16)


def three(product, left, right):
    return product(left[0], right[0]) + (product(left[0], right[1]) + product(left[1], right[0]))


def refit_kernel(place, count, peak, whole, master, updated, sent, held, gram_held):
    rows = master.shape[1]
    first = pl.multiple_of(place[0] * rows, rows)
    head = whole[...]
    current = head.astype(jnp.float32)
    square = jnp.sum(jnp.sum(current * current, axis=0, keepdims=True), axis=1, keepdims=True)
    scale = 1.0 / (jnp.sqrt(square) + epsilon)
    gram = dot_t(head, head) * scale * scale
    for iteration in range(ITERS - 1):
        pair = split(gram)
        poly = split(newton_b * gram + newton_c * three(dot, pair, pair))
        if iteration == 0:
            current = (newton_a * current + (dot(poly[0], head) + dot(poly[1], head))) * scale
        else:
            current = newton_a * current + three(dot, poly, halves)
        halves = split(current)
        gram = three(dot_t, halves, halves)
    held[...] = current
    gram_held[...] = gram
    gram_rows = gram_held[pl.ds(first, rows), :]
    poly = newton_b * gram_rows + newton_c * three(dot, split(gram_rows), split(gram))
    ortho = newton_a * held[pl.ds(first, rows), :] + three(dot, split(poly), halves)

    shape = ortho.shape
    gamma = jnp.where(count[0] > 0, clip_tau / jnp.full(shape, peak[0], jnp.float32), 1.0)
    row_index = first + lax.broadcasted_iota(jnp.int32, shape, 0)
    factor = jnp.where(row_index < K_NOPE, jnp.sqrt(gamma), 1.0)
    result = (
        (1.0 - learn_rate * decay_rate) * master[0] - learn_rate * 0.2 * math.sqrt(KVR) * ortho
    ) * factor
    updated[0] = result
    narrow = result.astype(jnp.bfloat16)
    places, _, width = sent.shape
    for device in range(places):
        part = device % 2 * 2 + device // (places // 2)
        sent[device] = narrow[:, part * width : (part + 1) * width]


def order_kernel(server_map, parts, ordered):
    slots = parts.shape[0]
    for slot in range(slots):
        part = parts[server_map[slot]]
        ordered[slot] = part
        ordered[slots + slot] = part


def join_kernel(core, own, other, serving, held, sems):
    sides, blocks, slots, rows, width = own.shape

    def fill(slot, lower, upper):
        for half, source in enumerate((lower, upper)):
            for side in range(sides):
                part = half * sides + side
                for block in range(blocks):
                    held[
                        slot, block * rows : (block + 1) * rows, part * width : (part + 1) * width
                    ] = source[side, block, slot]

    for slot in range(slots):

        @pl.when(core[0] == 0)
        def _():
            fill(slot, own, other)

        @pl.when(core[0] != 0)
        def _():
            fill(slot, other, own)

        pltpu.make_async_copy(held.at[slot], serving.at[slot], sems.at[slot]).start()
    for slot in range(slots):
        pltpu.make_async_copy(held.at[slot], serving.at[slot], sems.at[slot]).wait()


def shards(gradient, momentum, master, clip_count, logit_peak, server_map):
    new_momentum = momentum_mu * momentum + gradient
    nesterov = gradient + momentum_mu * new_momentum
    _, row_count, columns = gradient.shape
    shard_count = lax.axis_size(SHARD_AXIS)
    heads = server_map.shape[0]
    slots = heads // shard_count
    width = columns // PARTS
    shard_pos = lax.axis_index(SHARD_AXIS).astype(jnp.int32)[None]
    core_pos = lax.axis_index("core").astype(jnp.int32)[None]

    own_rows = jnp.broadcast_to(nesterov.astype(jnp.bfloat16), (shard_count, row_count, columns))
    whole_head = lax.all_to_all(own_rows, SHARD_AXIS, 0, 0, tiled=True)
    whole_head = whole_head.reshape(shard_count * row_count, columns)

    updated, sent = pl.pallas_call(
        refit_kernel,
        out_shape=(
            jax.ShapeDtypeStruct(master.shape, jnp.float32),
            jax.ShapeDtypeStruct((heads, row_count, width), jnp.bfloat16),
        ),
        in_specs=[SMEM, SMEM, SMEM, VMEM, VMEM],
        out_specs=(VMEM, VMEM),
        scratch_shapes=[
            pltpu.VMEM(whole_head.shape, jnp.float32),
            pltpu.VMEM((whole_head.shape[0],) * 2, jnp.float32),
        ],
    )(shard_pos, clip_count, logit_peak, whole_head, master)

    head_parts = lax.all_to_all(sent, HEAD_AXES, 0, 0, tiled=True)
    ordered = pl.pallas_call(
        order_kernel,
        out_shape=jax.ShapeDtypeStruct((2 * heads, row_count, width), jnp.bfloat16),
        in_specs=[SMEM, VMEM],
        out_specs=VMEM,
    )(server_map, head_parts)
    ordered = ordered.reshape(2 * shard_count, slots, row_count, width)
    own = lax.all_to_all(ordered, ("xh", SHARD_AXIS), 0, 0, tiled=True)
    own = own.reshape(2, shard_count, slots, row_count, width)
    other = lax.ppermute(own, "core", [(0, 1), (1, 0)])
    serving_shape = (slots, shard_count * row_count, columns)
    serving = pl.pallas_call(
        join_kernel,
        out_shape=jax.ShapeDtypeStruct(serving_shape, jnp.bfloat16),
        in_specs=[SMEM, VMEM, VMEM],
        out_specs=pl.BlockSpec(memory_space=pl.ANY),
        scratch_shapes=[
            pltpu.VMEM(serving_shape, jnp.bfloat16),
            pltpu.SemaphoreType.DMA((slots,)),
        ],
    )(core_pos, own, other)
    return (updated, new_momentum, serving)


def solution(mesh):
    side, grp, shard = (mesh.shape[name] for name in ("side", "grp", "shard"))
    fine = Mesh(
        mesh.devices.reshape(side, grp // 2, 2, shard), ("xh", "z", "core", "shard")
    )
    rows = P(HEAD_AXES, SHARD_AXIS, None)
    return jax.shard_map(
        shards,
        mesh=fine,
        in_specs=(rows, rows, rows, P(HEAD_AXES), P(HEAD_AXES), P()),
        out_specs=(rows, rows, P(SHARD_AXIS, None, None)),
        check_vma=False,
    )
```

```python
import math

import jax
import jax.numpy as jnp
from jax import lax
from jax.experimental import pallas as pl
from jax.experimental.pallas import tpu as pltpu
from jax.sharding import Mesh
from jax.sharding import PartitionSpec as P

KVR = 512
K_NOPE = 128
ITERS = 5


newton_a = 3.4445
newton_b = -4.775
newton_c = 2.0315
momentum_mu = 0.95
learn_rate = 0.5
decay_rate = 0.1
clip_tau = 100.0
epsilon = 1e-07

HEAD_AXES = ("xh", "z", "core")
SHARD_AXIS = "shard"
PARTS = 4

VMEM = pl.BlockSpec(memory_space=pltpu.VMEM)
SMEM = pl.BlockSpec(memory_space=pltpu.SMEM)
LARGE = pltpu.CompilerParams(vmem_limit_bytes=12 << 20)
SMALL = pltpu.CompilerParams(vmem_limit_bytes=6 << 20)


def dot(left, right):
    return jnp.dot(left, right, preferred_element_type=jnp.float32)


def dot_t(left, right):
    return lax.dot_general(
        left, right, (((1,), (1,)), ((), ())), preferred_element_type=jnp.float32
    )


def split(value):
    high = value.astype(jnp.bfloat16)
    return high, (value - high.astype(jnp.float32)).astype(jnp.bfloat16)


def three(product, left, right):
    return product(left[0], right[0]) + (product(left[0], right[1]) + product(left[1], right[0]))


def three_gram(pair, product):
    cross = product(pair[0], pair[1])
    return product(pair[0], pair[0]) + (cross + cross.T)


def refit_kernel(place, count, peak, whole, master, updated, sent, held, gram_held):
    rows = master.shape[1]
    first = pl.multiple_of(place[0] * rows, rows)
    head = whole[...]
    current = head.astype(jnp.float32)
    square = jnp.sum(jnp.sum(current * current, axis=0, keepdims=True), axis=1, keepdims=True)
    scale = 1.0 / (jnp.sqrt(square) + epsilon)
    gram = dot_t(head, head) * scale * scale
    for iteration in range(ITERS - 1):
        pair = split(gram)
        poly = split(newton_b * gram + newton_c * three_gram(pair, dot))
        if iteration == 0:
            current = (newton_a * current + (dot(poly[0], head) + dot(poly[1], head))) * scale
        else:
            current = newton_a * current + three(dot, poly, halves)
        halves = split(current)
        gram = three_gram(halves, dot_t)
    held[...] = current
    gram_held[...] = gram
    gram_rows = gram_held[pl.ds(first, rows), :]
    poly = newton_b * gram_rows + newton_c * three(dot, split(gram_rows), split(gram))
    ortho = newton_a * held[pl.ds(first, rows), :] + three(dot, split(poly), halves)

    shape = ortho.shape
    gamma = jnp.where(count[0] > 0, clip_tau / jnp.full(shape, peak[0], jnp.float32), 1.0)
    row_index = first + lax.broadcasted_iota(jnp.int32, shape, 0)
    factor = jnp.where(row_index < K_NOPE, jnp.sqrt(gamma), 1.0)
    result = (
        (1.0 - learn_rate * decay_rate) * master[0] - learn_rate * 0.2 * math.sqrt(KVR) * ortho
    ) * factor
    updated[0] = result
    narrow = result.astype(jnp.bfloat16)
    places, _, width = sent.shape
    for device in range(places):
        part = device % 2 * 2 + device // (places // 2)
        sent[device] = narrow[:, part * width : (part + 1) * width]


def order_kernel(server_map, parts, ordered):
    slots = parts.shape[0]
    for slot in range(slots):
        part = parts[server_map[slot]]
        ordered[slot] = part
        ordered[slots + slot] = part


def join_kernel(core, own, other, serving, held, sems):
    sides, blocks, slots, rows, width = own.shape

    def fill(slot, lower, upper):
        for half, source in enumerate((lower, upper)):
            for side in range(sides):
                part = half * sides + side
                for block in range(blocks):
                    held[
                        slot, block * rows : (block + 1) * rows, part * width : (part + 1) * width
                    ] = source[side, block, slot]

    for slot in range(slots):

        @pl.when(core[0] == 0)
        def _():
            fill(slot, own, other)

        @pl.when(core[0] != 0)
        def _():
            fill(slot, other, own)

        pltpu.make_async_copy(held.at[slot], serving.at[slot], sems.at[slot]).start()
    for slot in range(slots):
        pltpu.make_async_copy(held.at[slot], serving.at[slot], sems.at[slot]).wait()


def shards(gradient, momentum, master, clip_count, logit_peak, server_map):
    new_momentum = momentum_mu * momentum + gradient
    nesterov = gradient + momentum_mu * new_momentum
    _, row_count, columns = gradient.shape
    shard_count = lax.axis_size(SHARD_AXIS)
    heads = server_map.shape[0]
    slots = heads // shard_count
    width = columns // PARTS
    shard_pos = lax.axis_index(SHARD_AXIS).astype(jnp.int32)[None]
    core_pos = lax.axis_index("core").astype(jnp.int32)[None]

    own_rows = jnp.broadcast_to(nesterov.astype(jnp.bfloat16), (shard_count, row_count, columns))
    whole_head = lax.all_to_all(own_rows, SHARD_AXIS, 0, 0, tiled=True)
    whole_head = whole_head.reshape(shard_count * row_count, columns)

    updated, sent = pl.pallas_call(
        refit_kernel,
        out_shape=(
            jax.ShapeDtypeStruct(master.shape, jnp.float32),
            jax.ShapeDtypeStruct((heads, row_count, width), jnp.bfloat16),
        ),
        in_specs=[SMEM, SMEM, SMEM, VMEM, VMEM],
        out_specs=(VMEM, VMEM),
        scratch_shapes=[
            pltpu.VMEM(whole_head.shape, jnp.float32),
            pltpu.VMEM((whole_head.shape[0],) * 2, jnp.float32),
        ],
        compiler_params=LARGE,
    )(shard_pos, clip_count, logit_peak, whole_head, master)

    head_parts = lax.all_to_all(sent, HEAD_AXES, 0, 0, tiled=True)
    ordered = pl.pallas_call(
        order_kernel,
        out_shape=jax.ShapeDtypeStruct((2 * heads, row_count, width), jnp.bfloat16),
        in_specs=[SMEM, VMEM],
        out_specs=VMEM,
        compiler_params=SMALL,
    )(server_map, head_parts)
    ordered = ordered.reshape(2 * shard_count, slots, row_count, width)
    own = lax.all_to_all(ordered, ("xh", SHARD_AXIS), 0, 0, tiled=True)
    own = own.reshape(2, shard_count, slots, row_count, width)
    other = lax.ppermute(own, "core", [(0, 1), (1, 0)])
    serving_shape = (slots, shard_count * row_count, columns)
    serving = pl.pallas_call(
        join_kernel,
        out_shape=jax.ShapeDtypeStruct(serving_shape, jnp.bfloat16),
        in_specs=[SMEM, VMEM, VMEM],
        out_specs=pl.BlockSpec(memory_space=pl.ANY),
        scratch_shapes=[
            pltpu.VMEM(serving_shape, jnp.bfloat16),
            pltpu.SemaphoreType.DMA((slots,)),
        ],
        compiler_params=SMALL,
    )(core_pos, own, other)
    return (updated, new_momentum, serving)


def solution(mesh):
    side, grp, shard = (mesh.shape[name] for name in ("side", "grp", "shard"))
    fine = Mesh(
        mesh.devices.reshape(side, grp // 2, 2, shard), ("xh", "z", "core", "shard")
    )
    rows = P(HEAD_AXES, SHARD_AXIS, None)
    return jax.shard_map(
        shards,
        mesh=fine,
        in_specs=(rows, rows, rows, P(HEAD_AXES), P(HEAD_AXES), P()),
        out_specs=(rows, rows, P(SHARD_AXIS, None, None)),
        check_vma=False,
    )
```

```python
import math

import jax
import jax.numpy as jnp
from jax import lax
from jax.experimental import pallas as pl
from jax.experimental.pallas import tpu as pltpu
from jax.sharding import Mesh
from jax.sharding import PartitionSpec as P

KVR = 512
K_NOPE = 128
ITERS = 5


newton_a = 3.4445
newton_b = -4.775
newton_c = 2.0315
momentum_mu = 0.95
learn_rate = 0.5
decay_rate = 0.1
clip_tau = 100.0
epsilon = 1e-07

HEAD_AXES = ("xh", "zh", "zl", "core")
SHARD_AXIS = "shard"
SHARERS = ("xh", "zl")
PARTS = 4

VMEM = pl.BlockSpec(memory_space=pltpu.VMEM)
SMEM = pl.BlockSpec(memory_space=pltpu.SMEM)
LARGE = pltpu.CompilerParams(vmem_limit_bytes=12 << 20)
SMALL = pltpu.CompilerParams(vmem_limit_bytes=6 << 20)


def dot(left, right):
    return jnp.dot(left, right, preferred_element_type=jnp.float32)


def dot_t(left, right):
    return lax.dot_general(
        left, right, (((1,), (1,)), ((), ())), preferred_element_type=jnp.float32
    )


def split(value):
    high = value.astype(jnp.bfloat16)
    return high, (value - high.astype(jnp.float32)).astype(jnp.bfloat16)


def three(product, left, right):
    return product(left[0], right[0]) + (product(left[0], right[1]) + product(left[1], right[0]))


def three_gram(pair, product):
    cross = product(pair[0], pair[1])
    return product(pair[0], pair[0]) + (cross + cross.T)


def refit_kernel(place, count, peak, whole, master, updated, sent, held, gram_held):
    rows = master.shape[1]
    first = pl.multiple_of(place[0] * rows, rows)
    head = whole[...]
    current = head.astype(jnp.float32)
    square = jnp.sum(jnp.sum(current * current, axis=0, keepdims=True), axis=1, keepdims=True)
    scale = 1.0 / (jnp.sqrt(square) + epsilon)
    gram = dot_t(head, head) * scale * scale
    for iteration in range(ITERS - 1):
        pair = split(gram)
        poly = split(newton_b * gram + newton_c * three_gram(pair, dot))
        if iteration == 0:
            current = (newton_a * current + (dot(poly[0], head) + dot(poly[1], head))) * scale
        else:
            current = newton_a * current + three(dot, poly, halves)
        halves = split(current)
        gram = three_gram(halves, dot_t)
    held[...] = current
    gram_held[...] = gram
    gram_rows = gram_held[pl.ds(first, rows), :]
    poly = newton_b * gram_rows + newton_c * three(dot, split(gram_rows), split(gram))
    ortho = newton_a * held[pl.ds(first, rows), :] + three(dot, split(poly), halves)

    shape = ortho.shape
    gamma = jnp.where(count[0] > 0, clip_tau / jnp.full(shape, peak[0], jnp.float32), 1.0)
    row_index = first + lax.broadcasted_iota(jnp.int32, shape, 0)
    factor = jnp.where(row_index < K_NOPE, jnp.sqrt(gamma), 1.0)
    result = (
        (1.0 - learn_rate * decay_rate) * master[0] - learn_rate * 0.2 * math.sqrt(KVR) * ortho
    ) * factor
    updated[0] = result
    places, height, width = sent.shape
    narrow = [
        result[half * height : (half + 1) * height].astype(jnp.bfloat16) for half in range(2)
    ]
    for device in range(places):
        part = device % 2 * 2 + device // (places // 2)
        sent[device] = narrow[device // 2 % 2][:, part * width : (part + 1) * width]


def order_kernel(server_map, parts, ordered):
    for slot in range(parts.shape[0]):
        ordered[slot] = parts[server_map[slot]]


def join_kernel(core, own, other, serving, held, sems):
    sides, _, blocks, slots, height, width = own.shape
    rows = 2 * height

    def fill(slot, lower, upper):
        for half, source in enumerate((lower, upper)):
            for side in range(sides):
                part = half * sides + side
                for block in range(blocks):
                    held[
                        slot, block * rows : (block + 1) * rows, part * width : (part + 1) * width
                    ] = jnp.concatenate(
                        [source[side, 0, block, slot], source[side, 1, block, slot]], axis=0
                    )

    for slot in range(slots):

        @pl.when(core[0] == 0)
        def _():
            fill(slot, own, other)

        @pl.when(core[0] != 0)
        def _():
            fill(slot, other, own)

        pltpu.make_async_copy(held.at[slot], serving.at[slot], sems.at[slot]).start()
    for slot in range(slots):
        pltpu.make_async_copy(held.at[slot], serving.at[slot], sems.at[slot]).wait()


def shards(gradient, momentum, master, clip_count, logit_peak, server_map):
    new_momentum = momentum_mu * momentum + gradient
    nesterov = gradient + momentum_mu * new_momentum
    _, row_count, columns = gradient.shape
    shard_count = lax.axis_size(SHARD_AXIS)
    heads = server_map.shape[0]
    slots = heads // shard_count
    width, height = columns // PARTS, row_count // 2
    shard_pos = lax.axis_index(SHARD_AXIS).astype(jnp.int32)[None]
    core_pos = lax.axis_index("core").astype(jnp.int32)[None]

    own_rows = jnp.broadcast_to(nesterov.astype(jnp.bfloat16), (shard_count, row_count, columns))
    whole_head = lax.all_to_all(own_rows, SHARD_AXIS, 0, 0, tiled=True)
    whole_head = whole_head.reshape(shard_count * row_count, columns)

    updated, sent = pl.pallas_call(
        refit_kernel,
        out_shape=(
            jax.ShapeDtypeStruct(master.shape, jnp.float32),
            jax.ShapeDtypeStruct((heads, height, width), jnp.bfloat16),
        ),
        in_specs=[SMEM, SMEM, SMEM, VMEM, VMEM],
        out_specs=(VMEM, VMEM),
        scratch_shapes=[
            pltpu.VMEM(whole_head.shape, jnp.float32),
            pltpu.VMEM((whole_head.shape[0],) * 2, jnp.float32),
        ],
        compiler_params=LARGE,
    )(shard_pos, clip_count, logit_peak, whole_head, master)

    head_parts = lax.all_to_all(sent, HEAD_AXES, 0, 0, tiled=True)
    ordered = pl.pallas_call(
        order_kernel,
        out_shape=jax.ShapeDtypeStruct(head_parts.shape, jnp.bfloat16),
        in_specs=[SMEM, VMEM],
        out_specs=VMEM,
        compiler_params=SMALL,
    )(server_map, head_parts)
    ordered = ordered.reshape(shard_count, slots, height, width)
    own = lax.all_to_all(ordered, SHARD_AXIS, 0, 0, tiled=True)
    own = jnp.broadcast_to(own, (PARTS, *own.shape))
    own = lax.all_to_all(own, SHARERS, 0, 0, tiled=True)
    own = own.reshape(2, 2, shard_count, slots, height, width)
    other = lax.ppermute(own, "core", [(0, 1), (1, 0)])
    serving_shape = (slots, shard_count * row_count, columns)
    serving = pl.pallas_call(
        join_kernel,
        out_shape=jax.ShapeDtypeStruct(serving_shape, jnp.bfloat16),
        in_specs=[SMEM, VMEM, VMEM],
        out_specs=pl.BlockSpec(memory_space=pl.ANY),
        scratch_shapes=[
            pltpu.VMEM(serving_shape, jnp.bfloat16),
            pltpu.SemaphoreType.DMA((slots,)),
        ],
        compiler_params=SMALL,
    )(core_pos, own, other)
    return (updated, new_momentum, serving)


def solution(mesh):
    side, grp, shard = (mesh.shape[name] for name in ("side", "grp", "shard"))
    fine = Mesh(
        mesh.devices.reshape(side, grp // 4, 2, 2, shard), (*HEAD_AXES, SHARD_AXIS)
    )
    rows = P(HEAD_AXES, SHARD_AXIS, None)
    return jax.shard_map(
        shards,
        mesh=fine,
        in_specs=(rows, rows, rows, P(HEAD_AXES), P(HEAD_AXES), P()),
        out_specs=(rows, rows, P(SHARD_AXIS, None, None)),
        check_vma=False,
    )
```

```python
import math

import jax
import jax.numpy as jnp
from jax import lax
from jax.experimental import pallas as pl
from jax.experimental.pallas import tpu as pltpu
from jax.sharding import Mesh
from jax.sharding import PartitionSpec as P

KVR = 512
K_NOPE = 128
ITERS = 5


newton_a = 3.4445
newton_b = -4.775
newton_c = 2.0315
momentum_mu = 0.95
learn_rate = 0.5
decay_rate = 0.1
clip_tau = 100.0
epsilon = 1e-07

HEAD_AXES = ("xh", "zh", "zl", "core")
SHARD_AXIS = "shard"
SHARERS = ("xh", "zl")
PARTS = 4

VMEM = pl.BlockSpec(memory_space=pltpu.VMEM)
HBM = pl.BlockSpec(memory_space=pltpu.HBM)
SMEM = pl.BlockSpec(memory_space=pltpu.SMEM)
WHOLE = pltpu.CompilerParams(vmem_limit_bytes=60 << 20)
LARGE = pltpu.CompilerParams(vmem_limit_bytes=12 << 20)
SMALL = pltpu.CompilerParams(vmem_limit_bytes=6 << 20)


def dot(left, right):
    return jnp.dot(left, right, preferred_element_type=jnp.float32)


def dot_t(left, right):
    return lax.dot_general(
        left, right, (((1,), (1,)), ((), ())), preferred_element_type=jnp.float32
    )


def split(value):
    high = value.astype(jnp.bfloat16)
    return high, (value - high.astype(jnp.float32)).astype(jnp.bfloat16)


def three(product, left, right):
    return product(left[0], right[0]) + (product(left[0], right[1]) + product(left[1], right[0]))


def symmetric(pairs, product):
    main = sum(product(pair[0], pair[0]) for pair in pairs)
    cross = sum(product(pair[0], pair[1]) for pair in pairs)
    return main + (cross + cross.T)


def rows_kernel(gradient, momentum, own_rows, new_momentum, held, narrow, sems):
    loads = [
        pltpu.make_async_copy(source, held.at[place], sems.at[place])
        for place, source in enumerate((gradient, momentum))
    ]
    for load in loads:
        load.start()
    for load in loads:
        load.wait()
    value = held[0]
    moved = momentum_mu * held[1] + value
    narrow[...] = (value + momentum_mu * moved)[0].astype(jnp.bfloat16)
    held[1] = moved
    devices = own_rows.shape[0]
    stores = [
        pltpu.make_async_copy(narrow, own_rows.at[device], sems.at[2 + device])
        for device in range(devices)
    ]
    stores.append(pltpu.make_async_copy(held.at[1], new_momentum, sems.at[2 + devices]))
    for store in stores:
        store.start()
    for store in stores:
        store.wait()


def refit_kernel(place, count, peak, whole, master, updated, sent, held, gram_held):
    rows = master.shape[1]
    first = pl.multiple_of(place[0] * rows, rows)
    width = whole.shape[1] // 2
    blocks = [slice(block * width, (block + 1) * width) for block in range(2)]
    head = [whole[:, block] for block in blocks]
    current = [part.astype(jnp.float32) for part in head]
    square = sum(
        jnp.sum(jnp.sum(part * part, axis=0, keepdims=True), axis=1, keepdims=True)
        for part in current
    )
    scale = 1.0 / (jnp.sqrt(square) + epsilon)
    gram = sum(dot_t(part, part) for part in head) * scale * scale
    for iteration in range(ITERS - 1):
        pair = split(gram)
        poly = split(newton_b * gram + newton_c * symmetric([pair], dot))
        if iteration == 0:
            current = [
                (newton_a * old + (dot(poly[0], part) + dot(poly[1], part))) * scale
                for old, part in zip(current, head)
            ]
        else:
            current = [
                newton_a * old + three(dot, poly, part) for old, part in zip(current, halves)
            ]
        halves = [split(part) for part in current]
        gram = symmetric(halves, dot_t)
    for block, part in zip(blocks, current):
        held[:, block] = part
    gram_held[...] = gram
    gram_rows = gram_held[pl.ds(first, rows), :]
    poly = split(newton_b * gram_rows + newton_c * three(dot, split(gram_rows), split(gram)))
    turned = jnp.concatenate([three(dot, poly, part) for part in halves], axis=1)
    ortho = newton_a * held[pl.ds(first, rows), :] + turned

    shape = ortho.shape
    gamma = jnp.where(count[0] > 0, clip_tau / jnp.full(shape, peak[0], jnp.float32), 1.0)
    row_index = first + lax.broadcasted_iota(jnp.int32, shape, 0)
    factor = jnp.where(row_index < K_NOPE, jnp.sqrt(gamma), 1.0)
    result = (
        (1.0 - learn_rate * decay_rate) * master[0] - learn_rate * 0.2 * math.sqrt(KVR) * ortho
    ) * factor
    updated[0] = result
    places, height, width = sent.shape
    narrow = [
        result[half * height : (half + 1) * height].astype(jnp.bfloat16) for half in range(2)
    ]
    for device in range(places):
        part = device % 2 * 2 + device // (places // 2)
        sent[device] = narrow[device // 2 % 2][:, part * width : (part + 1) * width]


def order_kernel(server_map, parts, ordered):
    for slot in range(parts.shape[0]):
        ordered[slot] = parts[server_map[slot]]


def join_kernel(core, own, other, serving, held, sems):
    sides, _, blocks, slots, height, width = own.shape
    rows = 2 * height

    def fill(slot, lower, upper):
        for half, source in enumerate((lower, upper)):
            for side in range(sides):
                part = half * sides + side
                for block in range(blocks):
                    held[
                        slot, block * rows : (block + 1) * rows, part * width : (part + 1) * width
                    ] = jnp.concatenate(
                        [source[side, 0, block, slot], source[side, 1, block, slot]], axis=0
                    )

    for slot in range(slots):

        @pl.when(core[0] == 0)
        def _():
            fill(slot, own, other)

        @pl.when(core[0] != 0)
        def _():
            fill(slot, other, own)

        pltpu.make_async_copy(held.at[slot], serving.at[slot], sems.at[slot]).start()
    for slot in range(slots):
        pltpu.make_async_copy(held.at[slot], serving.at[slot], sems.at[slot]).wait()


def shards(gradient, momentum, master, clip_count, logit_peak, server_map):
    _, row_count, columns = gradient.shape
    shard_count = lax.axis_size(SHARD_AXIS)
    heads = server_map.shape[0]
    slots = heads // shard_count
    width, height = columns // PARTS, row_count // 2
    shard_pos = lax.axis_index(SHARD_AXIS).astype(jnp.int32)[None]
    core_pos = lax.axis_index("core").astype(jnp.int32)[None]

    own_rows, new_momentum = pl.pallas_call(
        rows_kernel,
        out_shape=(
            jax.ShapeDtypeStruct((shard_count, row_count, columns), jnp.bfloat16),
            jax.ShapeDtypeStruct(momentum.shape, jnp.float32),
        ),
        in_specs=[HBM, HBM],
        out_specs=(HBM, HBM),
        scratch_shapes=[
            pltpu.VMEM((2, *gradient.shape), jnp.float32),
            pltpu.VMEM((row_count, columns), jnp.bfloat16),
            pltpu.SemaphoreType.DMA((shard_count + 3,)),
        ],
        compiler_params=WHOLE,
    )(gradient, momentum)
    whole_head = lax.all_to_all(own_rows, SHARD_AXIS, 0, 0, tiled=True)
    whole_head = whole_head.reshape(shard_count * row_count, columns)

    updated, sent = pl.pallas_call(
        refit_kernel,
        out_shape=(
            jax.ShapeDtypeStruct(master.shape, jnp.float32),
            jax.ShapeDtypeStruct((heads, height, width), jnp.bfloat16),
        ),
        in_specs=[SMEM, SMEM, SMEM, VMEM, VMEM],
        out_specs=(VMEM, VMEM),
        scratch_shapes=[
            pltpu.VMEM(whole_head.shape, jnp.float32),
            pltpu.VMEM((whole_head.shape[0],) * 2, jnp.float32),
        ],
        compiler_params=LARGE,
    )(shard_pos, clip_count, logit_peak, whole_head, master)

    head_parts = lax.all_to_all(sent, HEAD_AXES, 0, 0, tiled=True)
    ordered = pl.pallas_call(
        order_kernel,
        out_shape=jax.ShapeDtypeStruct(head_parts.shape, jnp.bfloat16),
        in_specs=[SMEM, VMEM],
        out_specs=VMEM,
        compiler_params=SMALL,
    )(server_map, head_parts)
    ordered = ordered.reshape(shard_count, slots, height, width)
    own = lax.all_to_all(ordered, SHARD_AXIS, 0, 0, tiled=True)
    own = jnp.broadcast_to(own, (PARTS, *own.shape))
    own = lax.all_to_all(own, SHARERS, 0, 0, tiled=True)
    own = own.reshape(2, 2, shard_count, slots, height, width)
    other = lax.ppermute(own, "core", [(0, 1), (1, 0)])
    serving_shape = (slots, shard_count * row_count, columns)
    serving = pl.pallas_call(
        join_kernel,
        out_shape=jax.ShapeDtypeStruct(serving_shape, jnp.bfloat16),
        in_specs=[SMEM, VMEM, VMEM],
        out_specs=pl.BlockSpec(memory_space=pl.ANY),
        scratch_shapes=[
            pltpu.VMEM(serving_shape, jnp.bfloat16),
            pltpu.SemaphoreType.DMA((slots,)),
        ],
        compiler_params=SMALL,
    )(core_pos, own, other)
    return (updated, new_momentum, serving)


def solution(mesh):
    side, grp, shard = (mesh.shape[name] for name in ("side", "grp", "shard"))
    fine = Mesh(
        mesh.devices.reshape(side, grp // 4, 2, 2, shard), (*HEAD_AXES, SHARD_AXIS)
    )
    rows = P(HEAD_AXES, SHARD_AXIS, None)
    return jax.shard_map(
        shards,
        mesh=fine,
        in_specs=(rows, rows, rows, P(HEAD_AXES), P(HEAD_AXES), P()),
        out_specs=(rows, rows, P(SHARD_AXIS, None, None)),
        check_vma=False,
    )
```

```python
import math

import jax
import jax.numpy as jnp
from jax import lax
from jax.experimental import pallas as pl
from jax.experimental.pallas import tpu as pltpu
from jax.sharding import Mesh
from jax.sharding import PartitionSpec as P

KVR = 512
K_NOPE = 128
ITERS = 5


newton_a = 3.4445
newton_b = -4.775
newton_c = 2.0315
momentum_mu = 0.95
learn_rate = 0.5
decay_rate = 0.1
clip_tau = 100.0
epsilon = 1e-07

HEAD_AXES = ("xh", "zh", "zl", "core")
SHARD_AXIS = "shard"
SHARERS = ("xh", "zl")
PARTS = 4

VMEM = pl.BlockSpec(memory_space=pltpu.VMEM)
HBM = pl.BlockSpec(memory_space=pltpu.HBM)
SMEM = pl.BlockSpec(memory_space=pltpu.SMEM)
WHOLE = pltpu.CompilerParams(vmem_limit_bytes=60 << 20)
LARGE = pltpu.CompilerParams(vmem_limit_bytes=12 << 20)
SMALL = pltpu.CompilerParams(vmem_limit_bytes=6 << 20)


def dot(left, right):
    return jnp.dot(left, right, preferred_element_type=jnp.float32)


def dot_t(left, right):
    return lax.dot_general(
        left, right, (((1,), (1,)), ((), ())), preferred_element_type=jnp.float32
    )


def split(value):
    high = value.astype(jnp.bfloat16)
    return high, (value - high.astype(jnp.float32)).astype(jnp.bfloat16)


def three(product, left, right):
    return product(left[0], right[0]) + (product(left[0], right[1]) + product(left[1], right[0]))


def symmetric(pairs, product):
    main = sum(product(pair[0], pair[0]) for pair in pairs)
    cross = sum(product(pair[0], pair[1]) for pair in pairs)
    return main + (cross + cross.T)


def rows_kernel(gradient, momentum, own_rows, new_momentum, held, narrow, sems):
    loads = [
        pltpu.make_async_copy(source, held.at[place], sems.at[place])
        for place, source in enumerate((gradient, momentum))
    ]
    for load in loads:
        load.start()
    for load in loads:
        load.wait()
    value = held[0]
    moved = momentum_mu * held[1] + value
    narrow[...] = (value + momentum_mu * moved)[0].astype(jnp.bfloat16)
    held[1] = moved
    devices = own_rows.shape[0]
    stores = [
        pltpu.make_async_copy(narrow, own_rows.at[device], sems.at[2 + device])
        for device in range(devices)
    ]
    stores.append(pltpu.make_async_copy(held.at[1], new_momentum, sems.at[2 + devices]))
    for store in stores:
        store.start()
    for store in stores:
        store.wait()


def refit_kernel(place, count, peak, whole, master, updated, sent, held, gram_held):
    rows = master.shape[1]
    first = pl.multiple_of(place[0] * rows, rows)
    width = whole.shape[1] // 2
    blocks = [slice(block * width, (block + 1) * width) for block in range(2)]
    head = [whole[:, block] for block in blocks]
    current = [part.astype(jnp.float32) for part in head]
    square = sum(
        jnp.sum(jnp.sum(part * part, axis=0, keepdims=True), axis=1, keepdims=True)
        for part in current
    )
    scale = 1.0 / (jnp.sqrt(square) + epsilon)
    gram = sum(dot_t(part, part) for part in head) * scale * scale
    for iteration in range(ITERS - 1):
        pair = split(gram)
        poly = split(newton_b * gram + newton_c * symmetric([pair], dot))
        if iteration == 0:
            current = [
                (newton_a * old + (dot(poly[0], part) + dot(poly[1], part))) * scale
                for old, part in zip(current, head)
            ]
        else:
            current = [
                newton_a * old + three(dot, poly, part) for old, part in zip(current, halves)
            ]
        halves = [split(part) for part in current]
        gram = symmetric(halves, dot_t)
    for block, part in zip(blocks, current):
        held[:, block] = part
    gram_held[...] = gram
    gram_rows = gram_held[pl.ds(first, rows), :]
    poly = split(newton_b * gram_rows + newton_c * three(dot, split(gram_rows), split(gram)))
    turned = jnp.concatenate([three(dot, poly, part) for part in halves], axis=1)
    ortho = newton_a * held[pl.ds(first, rows), :] + turned

    shape = ortho.shape
    gamma = jnp.where(count[0] > 0, clip_tau / jnp.full(shape, peak[0], jnp.float32), 1.0)
    row_index = first + lax.broadcasted_iota(jnp.int32, shape, 0)
    factor = jnp.where(row_index < K_NOPE, jnp.sqrt(gamma), 1.0)
    result = (
        (1.0 - learn_rate * decay_rate) * master[0] - learn_rate * 0.2 * math.sqrt(KVR) * ortho
    ) * factor
    updated[0] = result
    places, height, width = sent.shape
    narrow = [
        result[half * height : (half + 1) * height].astype(jnp.bfloat16) for half in range(2)
    ]
    for device in range(places):
        part = device % 2 * 2 + device // (places // 2)
        sent[device] = narrow[device // 2 % 2][:, part * width : (part + 1) * width]


def order_kernel(server_map, parts, ordered):
    for slot in range(parts.shape[0]):
        part = parts[server_map[slot]]
        for sharer in range(ordered.shape[0]):
            ordered[sharer, slot] = part


def join_kernel(core, own, other, serving, held, sems):
    sides, _, blocks, slots, height, width = own.shape
    rows = 2 * height

    def fill(slot, lower, upper):
        for half, source in enumerate((lower, upper)):
            for side in range(sides):
                part = half * sides + side
                for block in range(blocks):
                    held[
                        slot, block * rows : (block + 1) * rows, part * width : (part + 1) * width
                    ] = jnp.concatenate(
                        [source[side, 0, block, slot], source[side, 1, block, slot]], axis=0
                    )

    for slot in range(slots):

        @pl.when(core[0] == 0)
        def _():
            fill(slot, own, other)

        @pl.when(core[0] != 0)
        def _():
            fill(slot, other, own)

        pltpu.make_async_copy(held.at[slot], serving.at[slot], sems.at[slot]).start()
    for slot in range(slots):
        pltpu.make_async_copy(held.at[slot], serving.at[slot], sems.at[slot]).wait()


def shards(gradient, momentum, master, clip_count, logit_peak, server_map):
    _, row_count, columns = gradient.shape
    shard_count = lax.axis_size(SHARD_AXIS)
    heads = server_map.shape[0]
    slots = heads // shard_count
    width, height = columns // PARTS, row_count // 2
    shard_pos = lax.axis_index(SHARD_AXIS).astype(jnp.int32)[None]
    core_pos = lax.axis_index("core").astype(jnp.int32)[None]

    own_rows, new_momentum = pl.pallas_call(
        rows_kernel,
        out_shape=(
            jax.ShapeDtypeStruct((shard_count, row_count, columns), jnp.bfloat16),
            jax.ShapeDtypeStruct(momentum.shape, jnp.float32),
        ),
        in_specs=[HBM, HBM],
        out_specs=(HBM, HBM),
        scratch_shapes=[
            pltpu.VMEM((2, *gradient.shape), jnp.float32),
            pltpu.VMEM((row_count, columns), jnp.bfloat16),
            pltpu.SemaphoreType.DMA((shard_count + 3,)),
        ],
        compiler_params=WHOLE,
    )(gradient, momentum)
    whole_head = lax.all_to_all(own_rows, SHARD_AXIS, 0, 0, tiled=True)
    whole_head = whole_head.reshape(shard_count * row_count, columns)

    updated, sent = pl.pallas_call(
        refit_kernel,
        out_shape=(
            jax.ShapeDtypeStruct(master.shape, jnp.float32),
            jax.ShapeDtypeStruct((heads, height, width), jnp.bfloat16),
        ),
        in_specs=[SMEM, SMEM, SMEM, VMEM, VMEM],
        out_specs=(VMEM, VMEM),
        scratch_shapes=[
            pltpu.VMEM(whole_head.shape, jnp.float32),
            pltpu.VMEM((whole_head.shape[0],) * 2, jnp.float32),
        ],
        compiler_params=LARGE,
    )(shard_pos, clip_count, logit_peak, whole_head, master)

    head_parts = lax.all_to_all(sent, HEAD_AXES, 0, 0, tiled=True)
    sharers = lax.axis_size(SHARERS)
    ordered = pl.pallas_call(
        order_kernel,
        out_shape=jax.ShapeDtypeStruct((sharers, *head_parts.shape), jnp.bfloat16),
        in_specs=[SMEM, VMEM],
        out_specs=VMEM,
        compiler_params=SMALL,
    )(server_map, head_parts)
    ordered = ordered.reshape(sharers * shard_count, slots, height, width)
    own = lax.all_to_all(ordered, (*SHARERS, SHARD_AXIS), 0, 0, tiled=True)
    own = own.reshape(2, 2, shard_count, slots, height, width)
    other = lax.ppermute(own, "core", [(0, 1), (1, 0)])
    serving_shape = (slots, shard_count * row_count, columns)
    serving = pl.pallas_call(
        join_kernel,
        out_shape=jax.ShapeDtypeStruct(serving_shape, jnp.bfloat16),
        in_specs=[SMEM, VMEM, VMEM],
        out_specs=pl.BlockSpec(memory_space=pl.ANY),
        scratch_shapes=[
            pltpu.VMEM(serving_shape, jnp.bfloat16),
            pltpu.SemaphoreType.DMA((slots,)),
        ],
        compiler_params=SMALL,
    )(core_pos, own, other)
    return (updated, new_momentum, serving)


def solution(mesh):
    side, grp, shard = (mesh.shape[name] for name in ("side", "grp", "shard"))
    fine = Mesh(
        mesh.devices.reshape(side, grp // 4, 2, 2, shard), (*HEAD_AXES, SHARD_AXIS)
    )
    rows = P(HEAD_AXES, SHARD_AXIS, None)
    return jax.shard_map(
        shards,
        mesh=fine,
        in_specs=(rows, rows, rows, P(HEAD_AXES), P(HEAD_AXES), P()),
        out_specs=(rows, rows, P(SHARD_AXIS, None, None)),
        check_vma=False,
    )
```

```python
import math

import jax
import jax.numpy as jnp
from jax import lax
from jax.experimental import pallas as pl
from jax.experimental.pallas import tpu as pltpu
from jax.sharding import Mesh
from jax.sharding import PartitionSpec as P

KVR = 512
K_NOPE = 128
ITERS = 5


newton_a = 3.4445
newton_b = -4.775
newton_c = 2.0315
momentum_mu = 0.95
learn_rate = 0.5
decay_rate = 0.1
clip_tau = 100.0
epsilon = 1e-07

HEAD_AXES = ("xh", "zh", "zl", "core")
SHARD_AXIS = "shard"
SHARERS = ("xh", "zl")
PARTS = 4

VMEM = pl.BlockSpec(memory_space=pltpu.VMEM)
HBM = pl.BlockSpec(memory_space=pltpu.HBM)
SMEM = pl.BlockSpec(memory_space=pltpu.SMEM)
WHOLE = pltpu.CompilerParams(vmem_limit_bytes=60 << 20)
LARGE = pltpu.CompilerParams(vmem_limit_bytes=12 << 20)
SMALL = pltpu.CompilerParams(vmem_limit_bytes=6 << 20)


def dot(left, right):
    return jnp.dot(left, right, preferred_element_type=jnp.float32)


def dot_t(left, right):
    return lax.dot_general(
        left, right, (((1,), (1,)), ((), ())), preferred_element_type=jnp.float32
    )


def split(value):
    high = value.astype(jnp.bfloat16)
    return high, (value - high.astype(jnp.float32)).astype(jnp.bfloat16)


def three(product, left, right):
    return product(left[0], right[0]) + (product(left[0], right[1]) + product(left[1], right[0]))


def symmetric(pairs, product):
    main = sum(product(pair[0], pair[0]) for pair in pairs)
    cross = sum(product(pair[0], pair[1]) for pair in pairs)
    return main + (cross + cross.T)


def rows_kernel(gradient, momentum, own_rows, new_momentum, held, narrow, sems):
    loads = [
        pltpu.make_async_copy(source, held.at[place], sems.at[place])
        for place, source in enumerate((gradient, momentum))
    ]
    for load in loads:
        load.start()
    for load in loads:
        load.wait()
    value = held[0]
    moved = momentum_mu * held[1] + value
    narrow[...] = (value + momentum_mu * moved)[0].astype(jnp.bfloat16)
    held[1] = moved
    devices = own_rows.shape[0]
    stores = [
        pltpu.make_async_copy(narrow, own_rows.at[device], sems.at[2 + device])
        for device in range(devices)
    ]
    stores.append(pltpu.make_async_copy(held.at[1], new_momentum, sems.at[2 + devices]))
    for store in stores:
        store.start()
    for store in stores:
        store.wait()


def refit_kernel(place, count, peak, whole, master, updated, sent, held, gram_held):
    rows = master.shape[1]
    first = pl.multiple_of(place[0] * rows, rows)
    width = whole.shape[1] // 2
    blocks = [slice(block * width, (block + 1) * width) for block in range(2)]
    head = [whole[:, block] for block in blocks]
    current = [part.astype(jnp.float32) for part in head]
    square = sum(
        jnp.sum(jnp.sum(part * part, axis=0, keepdims=True), axis=1, keepdims=True)
        for part in current
    )
    scale = 1.0 / (jnp.sqrt(square) + epsilon)
    gram = sum(dot_t(part, part) for part in head) * scale * scale
    for iteration in range(ITERS - 1):
        pair = split(gram)
        poly = split(newton_b * gram + newton_c * symmetric([pair], dot))
        if iteration == 0:
            current = [
                (newton_a * old + (dot(poly[0], part) + dot(poly[1], part))) * scale
                for old, part in zip(current, head)
            ]
        else:
            current = [
                newton_a * old + three(dot, poly, part) for old, part in zip(current, halves)
            ]
        halves = [split(part) for part in current]
        gram = symmetric(halves, dot_t)
    for block, part in zip(blocks, current):
        held[:, block] = part
    gram_held[...] = gram
    gram_rows = gram_held[pl.ds(first, rows), :]
    poly = split(newton_b * gram_rows + newton_c * three(dot, split(gram_rows), split(gram)))
    turned = jnp.concatenate([three(dot, poly, part) for part in halves], axis=1)
    ortho = newton_a * held[pl.ds(first, rows), :] + turned

    shape = ortho.shape
    gamma = jnp.where(count[0] > 0, clip_tau / jnp.full(shape, peak[0], jnp.float32), 1.0)
    row_index = first + lax.broadcasted_iota(jnp.int32, shape, 0)
    factor = jnp.where(row_index < K_NOPE, jnp.sqrt(gamma), 1.0)
    result = (
        (1.0 - learn_rate * decay_rate) * master[0] - learn_rate * 0.2 * math.sqrt(KVR) * ortho
    ) * factor
    updated[0] = result
    places, height, width = sent.shape
    narrow = [
        result[half * height : (half + 1) * height].astype(jnp.bfloat16) for half in range(2)
    ]
    for device in range(places):
        part = device % 2 * 2 + device // (places // 2)
        sent[device] = narrow[device // 2 % 2][:, part * width : (part + 1) * width]


def order_kernel(server_map, parts, ordered):
    for slot in range(parts.shape[0]):
        part = parts[server_map[slot]]
        for sharer in range(ordered.shape[0]):
            ordered[sharer, slot] = part


def fill_half(half, source, serving, held, sems):
    sides, _, blocks, slots, height, width = source.shape
    rows = 2 * height
    first = pl.multiple_of(half * (sides * width), sides * width)
    copies = []
    for slot in range(slots):
        for side in range(sides):
            for block in range(blocks):
                held[
                    slot, block * rows : (block + 1) * rows, side * width : (side + 1) * width
                ] = jnp.concatenate(
                    [source[side, 0, block, slot], source[side, 1, block, slot]], axis=0
                )
        copies.append(
            pltpu.make_async_copy(
                held.at[slot], serving.at[slot, :, pl.ds(first, sides * width)], sems.at[slot]
            )
        )
        copies[-1].start()
    for copy in copies:
        copy.wait()


def own_kernel(core, own, serving, held, sems):
    fill_half(core[0], own, serving, held, sems)


def other_kernel(core, other, updated, half_done, serving, new_master, held, sems):
    master_copy = pltpu.make_async_copy(updated, new_master, sems.at[other.shape[3]])
    master_copy.start()
    fill_half(1 - core[0], other, serving, held, sems)
    master_copy.wait()


def shards(gradient, momentum, master, clip_count, logit_peak, server_map):
    _, row_count, columns = gradient.shape
    shard_count = lax.axis_size(SHARD_AXIS)
    heads = server_map.shape[0]
    slots = heads // shard_count
    width, height = columns // PARTS, row_count // 2
    shard_pos = lax.axis_index(SHARD_AXIS).astype(jnp.int32)[None]
    core_pos = lax.axis_index("core").astype(jnp.int32)[None]

    own_rows, new_momentum = pl.pallas_call(
        rows_kernel,
        out_shape=(
            jax.ShapeDtypeStruct((shard_count, row_count, columns), jnp.bfloat16),
            jax.ShapeDtypeStruct(momentum.shape, jnp.float32),
        ),
        in_specs=[HBM, HBM],
        out_specs=(HBM, HBM),
        scratch_shapes=[
            pltpu.VMEM((2, *gradient.shape), jnp.float32),
            pltpu.VMEM((row_count, columns), jnp.bfloat16),
            pltpu.SemaphoreType.DMA((shard_count + 3,)),
        ],
        compiler_params=WHOLE,
    )(gradient, momentum)
    whole_head = lax.all_to_all(own_rows, SHARD_AXIS, 0, 0, tiled=True)
    whole_head = whole_head.reshape(shard_count * row_count, columns)

    updated, sent = pl.pallas_call(
        refit_kernel,
        out_shape=(
            jax.ShapeDtypeStruct(master.shape, jnp.float32),
            jax.ShapeDtypeStruct((heads, height, width), jnp.bfloat16),
        ),
        in_specs=[SMEM, SMEM, SMEM, VMEM, VMEM],
        out_specs=(VMEM, VMEM),
        scratch_shapes=[
            pltpu.VMEM(whole_head.shape, jnp.float32),
            pltpu.VMEM((whole_head.shape[0],) * 2, jnp.float32),
        ],
        compiler_params=LARGE,
    )(shard_pos, clip_count, logit_peak, whole_head, master)

    head_parts = lax.all_to_all(sent, HEAD_AXES, 0, 0, tiled=True)
    sharers = lax.axis_size(SHARERS)
    ordered = pl.pallas_call(
        order_kernel,
        out_shape=jax.ShapeDtypeStruct((sharers, *head_parts.shape), jnp.bfloat16),
        in_specs=[SMEM, VMEM],
        out_specs=VMEM,
        compiler_params=SMALL,
    )(server_map, head_parts)
    ordered = ordered.reshape(sharers * shard_count, slots, height, width)
    own = lax.all_to_all(ordered, (*SHARERS, SHARD_AXIS), 0, 0, tiled=True)
    own = own.reshape(2, 2, shard_count, slots, height, width)
    other = lax.ppermute(own, "core", [(0, 1), (1, 0)])
    serving_shape = jax.ShapeDtypeStruct(
        (slots, shard_count * row_count, columns), jnp.bfloat16
    )
    scratch = [
        pltpu.VMEM((slots, shard_count * row_count, columns // 2), jnp.bfloat16),
        pltpu.SemaphoreType.DMA((slots + 1,)),
    ]
    serving = pl.pallas_call(
        own_kernel,
        out_shape=serving_shape,
        in_specs=[SMEM, VMEM],
        out_specs=HBM,
        scratch_shapes=scratch,
        compiler_params=SMALL,
    )(core_pos, own)
    serving, new_master = pl.pallas_call(
        other_kernel,
        out_shape=(serving_shape, jax.ShapeDtypeStruct(updated.shape, jnp.float32)),
        in_specs=[SMEM, VMEM, VMEM, HBM],
        out_specs=(HBM, HBM),
        scratch_shapes=scratch,
        input_output_aliases={3: 0},
        compiler_params=SMALL,
    )(core_pos, other, updated, serving)
    return (new_master, new_momentum, serving)


def solution(mesh):
    side, grp, shard = (mesh.shape[name] for name in ("side", "grp", "shard"))
    fine = Mesh(
        mesh.devices.reshape(side, grp // 4, 2, 2, shard), (*HEAD_AXES, SHARD_AXIS)
    )
    rows = P(HEAD_AXES, SHARD_AXIS, None)
    return jax.shard_map(
        shards,
        mesh=fine,
        in_specs=(rows, rows, rows, P(HEAD_AXES), P(HEAD_AXES), P()),
        out_specs=(rows, rows, P(SHARD_AXIS, None, None)),
        check_vma=False,
    )
```

```python
import math

import jax
import jax.numpy as jnp
from jax import lax
from jax.experimental import pallas as pl
from jax.experimental.pallas import tpu as pltpu
from jax.sharding import Mesh
from jax.sharding import PartitionSpec as P

KVR = 512
K_NOPE = 128
ITERS = 5


newton_a = 3.4445
newton_b = -4.775
newton_c = 2.0315
momentum_mu = 0.95
learn_rate = 0.5
decay_rate = 0.1
clip_tau = 100.0
epsilon = 1e-07

HEAD_AXES = ("xh", "zh", "zl", "core")
SHARD_AXIS = "shard"
SHARERS = ("xh", "zl")
PARTS = 4

VMEM = pl.BlockSpec(memory_space=pltpu.VMEM)
HBM = pl.BlockSpec(memory_space=pltpu.HBM)
SMEM = pl.BlockSpec(memory_space=pltpu.SMEM)
WHOLE = pltpu.CompilerParams(vmem_limit_bytes=60 << 20)
LARGE = pltpu.CompilerParams(vmem_limit_bytes=12 << 20)
SMALL = pltpu.CompilerParams(vmem_limit_bytes=6 << 20)


def dot(left, right):
    return jnp.dot(left, right, preferred_element_type=jnp.float32)


def dot_t(left, right):
    return lax.dot_general(
        left, right, (((1,), (1,)), ((), ())), preferred_element_type=jnp.float32
    )


def split(value):
    high = value.astype(jnp.bfloat16)
    return high, (value - high.astype(jnp.float32)).astype(jnp.bfloat16)


def three(product, left, right):
    return product(left[0], right[0]) + (product(left[0], right[1]) + product(left[1], right[0]))


def symmetric(pairs, product):
    main = sum(product(pair[0], pair[0]) for pair in pairs)
    cross = sum(product(pair[0], pair[1]) for pair in pairs)
    return main + (cross + cross.T)


def rows_kernel(gradient, momentum, own_rows, new_momentum, held, narrow, sems):
    loads = [
        pltpu.make_async_copy(source, held.at[place], sems.at[place])
        for place, source in enumerate((gradient, momentum))
    ]
    for load in loads:
        load.start()
    for load in loads:
        load.wait()
    value = held[0]
    moved = momentum_mu * held[1] + value
    narrow[...] = (value + momentum_mu * moved)[0].astype(jnp.bfloat16)
    held[1] = moved
    devices = own_rows.shape[0]
    stores = [
        pltpu.make_async_copy(narrow, own_rows.at[device], sems.at[2 + device])
        for device in range(devices)
    ]
    stores.append(pltpu.make_async_copy(held.at[1], new_momentum, sems.at[2 + devices]))
    for store in stores:
        store.start()
    for store in stores:
        store.wait()


def refit_kernel(count, peak, whole, master, updated, sent, held, gram_held):
    rows = master.shape[1]
    first = pl.multiple_of(lax.axis_index(SHARD_AXIS) * rows, rows)
    width = whole.shape[1] // 2
    blocks = [slice(block * width, (block + 1) * width) for block in range(2)]
    head = [whole[:, block] for block in blocks]
    current = [part.astype(jnp.float32) for part in head]
    square = sum(
        jnp.sum(jnp.sum(part * part, axis=0, keepdims=True), axis=1, keepdims=True)
        for part in current
    )
    scale = 1.0 / (jnp.sqrt(square) + epsilon)
    gram = sum(dot_t(part, part) for part in head) * scale * scale
    for iteration in range(ITERS - 1):
        pair = split(gram)
        poly = split(newton_b * gram + newton_c * symmetric([pair], dot))
        if iteration == 0:
            current = [
                (newton_a * old + (dot(poly[0], part) + dot(poly[1], part))) * scale
                for old, part in zip(current, head)
            ]
        else:
            current = [
                newton_a * old + three(dot, poly, part) for old, part in zip(current, halves)
            ]
        halves = [split(part) for part in current]
        gram = symmetric(halves, dot_t)
    for block, part in zip(blocks, current):
        held[:, block] = part
    gram_held[...] = gram
    gram_rows = gram_held[pl.ds(first, rows), :]
    poly = split(newton_b * gram_rows + newton_c * three(dot, split(gram_rows), split(gram)))
    turned = jnp.concatenate([three(dot, poly, part) for part in halves], axis=1)
    ortho = newton_a * held[pl.ds(first, rows), :] + turned

    shape = ortho.shape
    gamma = jnp.where(count[0] > 0, clip_tau / jnp.full(shape, peak[0], jnp.float32), 1.0)
    row_index = first + lax.broadcasted_iota(jnp.int32, shape, 0)
    factor = jnp.where(row_index < K_NOPE, jnp.sqrt(gamma), 1.0)
    result = (
        (1.0 - learn_rate * decay_rate) * master[0] - learn_rate * 0.2 * math.sqrt(KVR) * ortho
    ) * factor
    updated[0] = result
    places, height, width = sent.shape
    narrow = [
        result[half * height : (half + 1) * height].astype(jnp.bfloat16) for half in range(2)
    ]
    for device in range(places):
        part = device % 2 * 2 + device // (places // 2)
        sent[device] = narrow[device // 2 % 2][:, part * width : (part + 1) * width]


def order_kernel(server_map, parts, ordered):
    for slot in range(parts.shape[0]):
        part = parts[server_map[slot]]
        for sharer in range(ordered.shape[0]):
            ordered[sharer, slot] = part


def fill_half(half, source, serving, held, sems):
    sides, _, blocks, slots, height, width = source.shape
    rows = 2 * height
    first = pl.multiple_of(half * (sides * width), sides * width)
    copies = []
    for slot in range(slots):
        for side in range(sides):
            for block in range(blocks):
                held[
                    slot, block * rows : (block + 1) * rows, side * width : (side + 1) * width
                ] = jnp.concatenate(
                    [source[side, 0, block, slot], source[side, 1, block, slot]], axis=0
                )
        copies.append(
            pltpu.make_async_copy(
                held.at[slot], serving.at[slot, :, pl.ds(first, sides * width)], sems.at[slot]
            )
        )
        copies[-1].start()
    for copy in copies:
        copy.wait()


def own_kernel(own, serving, held, sems):
    fill_half(lax.axis_index("core"), own, serving, held, sems)


def other_kernel(other, updated, half_done, serving, new_master, held, sems):
    master_copy = pltpu.make_async_copy(updated, new_master, sems.at[other.shape[3]])
    master_copy.start()
    fill_half(1 - lax.axis_index("core"), other, serving, held, sems)
    master_copy.wait()


def shards(gradient, momentum, master, clip_count, logit_peak, server_map):
    _, row_count, columns = gradient.shape
    shard_count = lax.axis_size(SHARD_AXIS)
    heads = server_map.shape[0]
    slots = heads // shard_count
    width, height = columns // PARTS, row_count // 2

    own_rows, new_momentum = pl.pallas_call(
        rows_kernel,
        out_shape=(
            jax.ShapeDtypeStruct((shard_count, row_count, columns), jnp.bfloat16),
            jax.ShapeDtypeStruct(momentum.shape, jnp.float32),
        ),
        in_specs=[HBM, HBM],
        out_specs=(HBM, HBM),
        scratch_shapes=[
            pltpu.VMEM((2, *gradient.shape), jnp.float32),
            pltpu.VMEM((row_count, columns), jnp.bfloat16),
            pltpu.SemaphoreType.DMA((shard_count + 3,)),
        ],
        compiler_params=WHOLE,
    )(gradient, momentum)
    whole_head = lax.all_to_all(own_rows, SHARD_AXIS, 0, 0, tiled=True)
    whole_head = whole_head.reshape(shard_count * row_count, columns)

    updated, sent = pl.pallas_call(
        refit_kernel,
        out_shape=(
            jax.ShapeDtypeStruct(master.shape, jnp.float32),
            jax.ShapeDtypeStruct((heads, height, width), jnp.bfloat16),
        ),
        in_specs=[SMEM, SMEM, VMEM, VMEM],
        out_specs=(VMEM, VMEM),
        scratch_shapes=[
            pltpu.VMEM(whole_head.shape, jnp.float32),
            pltpu.VMEM((whole_head.shape[0],) * 2, jnp.float32),
        ],
        compiler_params=LARGE,
    )(clip_count, logit_peak, whole_head, master)

    head_parts = lax.all_to_all(sent, HEAD_AXES, 0, 0, tiled=True)
    sharers = lax.axis_size(SHARERS)
    ordered = pl.pallas_call(
        order_kernel,
        out_shape=jax.ShapeDtypeStruct((sharers, *head_parts.shape), jnp.bfloat16),
        in_specs=[SMEM, VMEM],
        out_specs=VMEM,
        compiler_params=SMALL,
    )(server_map, head_parts)
    ordered = ordered.reshape(sharers * shard_count, slots, height, width)
    own = lax.all_to_all(ordered, (*SHARERS, SHARD_AXIS), 0, 0, tiled=True)
    own = own.reshape(2, 2, shard_count, slots, height, width)
    other = lax.ppermute(own, "core", [(0, 1), (1, 0)])
    serving_shape = jax.ShapeDtypeStruct(
        (slots, shard_count * row_count, columns), jnp.bfloat16
    )
    scratch = [
        pltpu.VMEM((slots, shard_count * row_count, columns // 2), jnp.bfloat16),
        pltpu.SemaphoreType.DMA((slots + 1,)),
    ]
    serving = pl.pallas_call(
        own_kernel,
        out_shape=serving_shape,
        in_specs=[VMEM],
        out_specs=HBM,
        scratch_shapes=scratch,
        compiler_params=SMALL,
    )(own)
    serving, new_master = pl.pallas_call(
        other_kernel,
        out_shape=(serving_shape, jax.ShapeDtypeStruct(updated.shape, jnp.float32)),
        in_specs=[VMEM, VMEM, HBM],
        out_specs=(HBM, HBM),
        scratch_shapes=scratch,
        input_output_aliases={2: 0},
        compiler_params=SMALL,
    )(other, updated, serving)
    return (new_master, new_momentum, serving)


def solution(mesh):
    side, grp, shard = (mesh.shape[name] for name in ("side", "grp", "shard"))
    fine = Mesh(
        mesh.devices.reshape(side, grp // 4, 2, 2, shard), (*HEAD_AXES, SHARD_AXIS)
    )
    rows = P(HEAD_AXES, SHARD_AXIS, None)
    return jax.shard_map(
        shards,
        mesh=fine,
        in_specs=(rows, rows, rows, P(HEAD_AXES), P(HEAD_AXES), P()),
        out_specs=(rows, rows, P(SHARD_AXIS, None, None)),
        check_vma=False,
    )
```

```python
import math

import jax
import jax.numpy as jnp
from jax import lax
from jax.experimental import pallas as pl
from jax.experimental.pallas import tpu as pltpu
from jax.sharding import Mesh
from jax.sharding import PartitionSpec as P

KVR = 512
K_NOPE = 128
ITERS = 5


newton_a = 3.4445
newton_b = -4.775
newton_c = 2.0315
momentum_mu = 0.95
learn_rate = 0.5
decay_rate = 0.1
clip_tau = 100.0
epsilon = 1e-07

HEAD_AXES = ("xh", "zh", "zl", "core")
SHARD_AXIS = "shard"
SHARERS = ("xh", "zl")
PARTS = 4

VMEM = pl.BlockSpec(memory_space=pltpu.VMEM)
HBM = pl.BlockSpec(memory_space=pltpu.HBM)
SMEM = pl.BlockSpec(memory_space=pltpu.SMEM)
WHOLE = pltpu.CompilerParams(vmem_limit_bytes=60 << 20)
LARGE = pltpu.CompilerParams(vmem_limit_bytes=12 << 20)
SMALL = pltpu.CompilerParams(vmem_limit_bytes=6 << 20)


def dot(left, right):
    return jnp.dot(left, right, preferred_element_type=jnp.float32)


def dot_t(left, right):
    return lax.dot_general(
        left, right, (((1,), (1,)), ((), ())), preferred_element_type=jnp.float32
    )


def split(value):
    high = value.astype(jnp.bfloat16)
    return high, (value - high.astype(jnp.float32)).astype(jnp.bfloat16)


def three(product, left, right):
    return product(left[0], right[0]) + (product(left[0], right[1]) + product(left[1], right[0]))


def symmetric(pairs, product):
    main = sum(product(pair[0], pair[0]) for pair in pairs)
    cross = sum(product(pair[0], pair[1]) for pair in pairs)
    return main + (cross + cross.T)


def rows_kernel(gradient, momentum, own_rows, new_momentum, held, narrow, sems):
    loads = [
        pltpu.make_async_copy(source, held.at[place], sems.at[place])
        for place, source in enumerate((gradient, momentum))
    ]
    for load in loads:
        load.start()
    for load in loads:
        load.wait()
    value = held[0]
    moved = momentum_mu * held[1] + value
    narrow[...] = (value + momentum_mu * moved)[0].astype(jnp.bfloat16)
    held[1] = moved
    devices = own_rows.shape[0]
    stores = [
        pltpu.make_async_copy(narrow, own_rows.at[device], sems.at[2 + device])
        for device in range(devices)
    ]
    stores.append(pltpu.make_async_copy(held.at[1], new_momentum, sems.at[2 + devices]))
    for store in stores:
        store.start()
    for store in stores:
        store.wait()


def refit_kernel(count, peak, whole, master, updated, sent, held, gram_held):
    rows = master.shape[1]
    first = pl.multiple_of(lax.axis_index(SHARD_AXIS) * rows, rows)
    width = whole.shape[1] // 2
    blocks = [slice(block * width, (block + 1) * width) for block in range(2)]
    head = [whole[:, block] for block in blocks]
    current = [part.astype(jnp.float32) for part in head]
    square = sum(
        jnp.sum(jnp.sum(part * part, axis=0, keepdims=True), axis=1, keepdims=True)
        for part in current
    )
    scale = 1.0 / (jnp.sqrt(square) + epsilon)
    gram = sum(dot_t(part, part) for part in head) * scale * scale
    for iteration in range(ITERS - 1):
        pair = split(gram)
        poly = split(newton_b * gram + newton_c * symmetric([pair], dot))
        if iteration == 0:
            current = [
                (newton_a * old + (dot(poly[0], part) + dot(poly[1], part))) * scale
                for old, part in zip(current, head)
            ]
        else:
            current = [
                newton_a * old + three(dot, poly, part) for old, part in zip(current, halves)
            ]
        halves = [split(part) for part in current]
        gram = symmetric(halves, dot_t)
    for block, part in zip(blocks, current):
        held[:, block] = part
    gram_held[...] = gram
    gram_rows = gram_held[pl.ds(first, rows), :]
    poly = split(newton_b * gram_rows + newton_c * three(dot, split(gram_rows), split(gram)))
    turned = jnp.concatenate([three(dot, poly, part) for part in halves], axis=1)
    ortho = newton_a * held[pl.ds(first, rows), :] + turned

    shape = ortho.shape
    gamma = jnp.where(count[0] > 0, clip_tau / jnp.full(shape, peak[0], jnp.float32), 1.0)
    row_index = first + lax.broadcasted_iota(jnp.int32, shape, 0)
    factor = jnp.where(row_index < K_NOPE, jnp.sqrt(gamma), 1.0)
    result = (
        (1.0 - learn_rate * decay_rate) * master[0] - learn_rate * 0.2 * math.sqrt(KVR) * ortho
    ) * factor
    updated[0] = result
    places, height, width = sent.shape
    narrow = [
        result[half * height : (half + 1) * height].astype(jnp.bfloat16) for half in range(2)
    ]
    for device in range(places):
        part = device % 2 * 2 + device // (places // 2)
        sent[device] = narrow[device // 2 % 2][:, part * width : (part + 1) * width]


def order_kernel(server_map, parts, ordered):
    for slot in range(parts.shape[0]):
        part = parts[server_map[slot]]
        for sharer in range(ordered.shape[0]):
            ordered[sharer, slot] = part


def fill_half(half, source, serving, held, sems):
    sides, _, blocks, slots, height, width = source.shape
    rows = 2 * height
    first = pl.multiple_of(half * (sides * width), sides * width)
    copies = []
    for slot in range(slots):
        for side in range(sides):
            for block in range(blocks):
                held[
                    slot, block * rows : (block + 1) * rows, side * width : (side + 1) * width
                ] = jnp.concatenate(
                    [source[side, 0, block, slot], source[side, 1, block, slot]], axis=0
                )
        copies.append(
            pltpu.make_async_copy(
                held.at[slot], serving.at[slot, :, pl.ds(first, sides * width)], sems.at[slot]
            )
        )
        copies[-1].start()
    for copy in copies:
        copy.wait()


def own_kernel(own, updated, serving, new_master, held, sems):
    master_copy = pltpu.make_async_copy(updated, new_master, sems.at[own.shape[3]])
    master_copy.start()
    fill_half(lax.axis_index("core"), own, serving, held, sems)
    master_copy.wait()


def other_kernel(other, half_done, serving, held, sems):
    fill_half(1 - lax.axis_index("core"), other, serving, held, sems)


def shards(gradient, momentum, master, clip_count, logit_peak, server_map):
    _, row_count, columns = gradient.shape
    shard_count = lax.axis_size(SHARD_AXIS)
    heads = server_map.shape[0]
    slots = heads // shard_count
    width, height = columns // PARTS, row_count // 2

    own_rows, new_momentum = pl.pallas_call(
        rows_kernel,
        out_shape=(
            jax.ShapeDtypeStruct((shard_count, row_count, columns), jnp.bfloat16),
            jax.ShapeDtypeStruct(momentum.shape, jnp.float32),
        ),
        in_specs=[HBM, HBM],
        out_specs=(HBM, HBM),
        scratch_shapes=[
            pltpu.VMEM((2, *gradient.shape), jnp.float32),
            pltpu.VMEM((row_count, columns), jnp.bfloat16),
            pltpu.SemaphoreType.DMA((shard_count + 3,)),
        ],
        compiler_params=WHOLE,
    )(gradient, momentum)
    whole_head = lax.all_to_all(own_rows, SHARD_AXIS, 0, 0, tiled=True)
    whole_head = whole_head.reshape(shard_count * row_count, columns)

    updated, sent = pl.pallas_call(
        refit_kernel,
        out_shape=(
            jax.ShapeDtypeStruct(master.shape, jnp.float32),
            jax.ShapeDtypeStruct((heads, height, width), jnp.bfloat16),
        ),
        in_specs=[SMEM, SMEM, VMEM, VMEM],
        out_specs=(VMEM, VMEM),
        scratch_shapes=[
            pltpu.VMEM(whole_head.shape, jnp.float32),
            pltpu.VMEM((whole_head.shape[0],) * 2, jnp.float32),
        ],
        compiler_params=LARGE,
    )(clip_count, logit_peak, whole_head, master)

    head_parts = lax.all_to_all(sent, HEAD_AXES, 0, 0, tiled=True)
    sharers = lax.axis_size(SHARERS)
    ordered = pl.pallas_call(
        order_kernel,
        out_shape=jax.ShapeDtypeStruct((sharers, *head_parts.shape), jnp.bfloat16),
        in_specs=[SMEM, VMEM],
        out_specs=VMEM,
        compiler_params=SMALL,
    )(server_map, head_parts)
    ordered = ordered.reshape(sharers * shard_count, slots, height, width)
    own = lax.all_to_all(ordered, (*SHARERS, SHARD_AXIS), 0, 0, tiled=True)
    own = own.reshape(2, 2, shard_count, slots, height, width)
    other = lax.ppermute(own, "core", [(0, 1), (1, 0)])
    serving_shape = jax.ShapeDtypeStruct(
        (slots, shard_count * row_count, columns), jnp.bfloat16
    )
    scratch = [
        pltpu.VMEM((slots, shard_count * row_count, columns // 2), jnp.bfloat16),
        pltpu.SemaphoreType.DMA((slots + 1,)),
    ]
    serving, new_master = pl.pallas_call(
        own_kernel,
        out_shape=(serving_shape, jax.ShapeDtypeStruct(updated.shape, jnp.float32)),
        in_specs=[VMEM, VMEM],
        out_specs=(HBM, HBM),
        scratch_shapes=scratch,
        compiler_params=SMALL,
    )(own, updated)
    serving = pl.pallas_call(
        other_kernel,
        out_shape=serving_shape,
        in_specs=[VMEM, HBM],
        out_specs=HBM,
        scratch_shapes=scratch,
        input_output_aliases={1: 0},
        compiler_params=SMALL,
    )(other, serving)
    return (new_master, new_momentum, serving)


def solution(mesh):
    side, grp, shard = (mesh.shape[name] for name in ("side", "grp", "shard"))
    fine = Mesh(
        mesh.devices.reshape(side, grp // 4, 2, 2, shard), (*HEAD_AXES, SHARD_AXIS)
    )
    rows = P(HEAD_AXES, SHARD_AXIS, None)
    return jax.shard_map(
        shards,
        mesh=fine,
        in_specs=(rows, rows, rows, P(HEAD_AXES), P(HEAD_AXES), P()),
        out_specs=(rows, rows, P(SHARD_AXIS, None, None)),
        check_vma=False,
    )
```
